128 devices in a mesh: date: 4 (over y), tile: 32 (over x, z, core).
Axes of the slice: x: 4, y: 4, z: 4, core: 2. Of those that a mesh axis runs over, the one named last changes fastest.
Arguments:
- swath_intensities: bfloat16 [4, 512, 64, 2, 512], P('date', 'tile'), may hold values from 0.0099487305 to 1
- destination_patch: int32 [512, 1], P('tile'), may hold values from 0 to 31; in each aligned block of 16 rows (0 to 15, 16 to 31, ...) at most 2 rows name the same one
- swath_leading_scanline: int32 [512], P('tile'), may hold values from 0 to 64
- receiver_floor_intensity: float32 [4, 4096, 2, 512], P('date', 'tile'), may hold values from 0.1 to 1
Outputs:
- filtered: bfloat16 [4, 4096, 2, 512], P('date', 'tile')
The draws below stay inside these ranges and needn't reach their ends.
Inputs may be any that keep to these rules, and one draw needn't show every extreme that they name: `destination_patch`: among the 16 blocks of one device no owner is named more than 2 times.
All inputs are finite; a program needn't handle non-finite values.
Results may differ from the reference program's by a relative error of at most 0.008.
Values may be sent and summed in bfloat16 or wider, within the bound.
A program may use at most 128 MiB of HBM per device.

```python
import math
import jax
import jax.numpy as jnp
import numpy as np
from jax import lax

RASTER_BREADTH = 512
SWATH_HEIGHT = 64
PATCH_HEIGHT = 128
SWATHS_HELD = 16
SHIPMENT_BOUND = 2
SWATHS_ALTOGETHER = 512
PASSES_ALTOGETHER = 4
N_TILE = 32


def touch_ends(array, stream_key, smallest, high):
    index_at = [jax.random.randint(jax.random.fold_in(stream_key, axis), (), 0, length) for axis, length in enumerate(array.shape)]
    longest = array.shape.index(max(array.shape))
    next_to = index_at[:longest] + [(index_at[longest] + 1) % array.shape[longest]] + index_at[longest + 1:]
    return array.at[tuple(index_at)].set(smallest).at[tuple(next_to)].set(high)


def level_of(own_key, extent, pieces, smallest, largest):
    level, own = 1.0, jax.random.fold_in(own_key, 6)
    for dim, blocks in pieces:
        steps = jnp.exp(jax.random.uniform(jax.random.fold_in(own, dim), (blocks,), jnp.float32, smallest / len(pieces), largest / len(pieces)))
        level = level * jnp.repeat(steps, extent[dim] // blocks).reshape([-1 if axis == dim else 1 for axis in range(len(extent))])
    return level


def shared_out(stream_key, own, number, rows, number_of, top, most, lean):
    order = jax.random.permutation(stream_key, number_of)
    heavy_load, usual = load_shares(number_of, rows * top, most, lean, True), load_shares(number_of, rows * top, most, lean, False)
    places = jnp.arange(number_of)

    def named(lengths, turn):
        used = int((lengths > 0).sum())
        fixed = max(1, used // 4)
        moved = fixed + (places - fixed + turn * (used - fixed)) % max(1, number_of - fixed)
        return jnp.zeros((number_of,), jnp.int32).at[order[jnp.where(places < fixed, places, moved)]].set(jnp.asarray(lengths, jnp.int32))

    lengths = jnp.where(number % 4 == 0, named(heavy_load, number // 4), named(usual, number - number // 4 - 1))
    mixed = jax.random.permutation(jax.random.fold_in(own, 3), number_of)
    donor, taker = mixed[0:number_of // 2 * 2:2], mixed[1:number_of // 2 * 2:2]
    slack = jnp.minimum(lengths[donor] - 1, most - lengths[taker]) // 2
    slack = jnp.where((donor == order[0]) | (taker == order[0]) | (lengths[taker] == 0), 0, jnp.maximum(slack, 0))
    moved = jax.random.randint(jax.random.fold_in(own, 4), (number_of // 2,), 0, 1 << 20) % (slack + 1)
    lengths = lengths.at[donor].add(-moved).at[taker].add(moved)
    labels = jnp.searchsorted(jnp.cumsum(lengths), jnp.arange(rows * top), side="right").astype(jnp.int32)
    table = labels.reshape(top, rows).T
    table = table[jax.random.permutation(jax.random.fold_in(own, 1), rows)]
    turn = jax.random.randint(jax.random.fold_in(own, 2), (rows, 1), 0, top)
    return jnp.take_along_axis(table, (jnp.arange(top)[None, :] + turn) % top, axis=1)


def load_shares(amount, total, reach, skew, full):
    loads = [(1 << 20) // math.isqrt(grade ** skew) + 1 for grade in range(1, amount + 1)]
    largest = reach if full else min(reach, max(-(-total // amount), total * loads[0] // sum(loads)))
    least = 1 if total - largest >= amount - 1 else 0
    holding, spare = [largest] + [least] * (amount - 1), total - largest - least * (amount - 1)
    while spare > 0:
        candidates = [i for i in range(1, amount) if holding[i] < largest] or [i for i in range(1, amount) if holding[i] < reach]
        pool, remaining = sum([loads[i] for i in candidates]), spare
        for i in candidates:
            extra = min(reach - holding[i], max(1, remaining * loads[i] // pool), spare)
            holding[i] = holding[i] + extra
            spare = spare - extra
    return np.array(holding)


def setup_inputs(seed: int = 0) -> dict:
    splits = jax.random.split(jax.random.key(seed), 5)
    swath_intensities = jnp.clip(jnp.exp(math.log(1.0) - 4.61031033 * jax.random.uniform(splits[0], (PASSES_ALTOGETHER, SWATHS_ALTOGETHER, SWATH_HEIGHT, 2, RASTER_BREADTH), jnp.float32) ** level_of(splits[0], (PASSES_ALTOGETHER, SWATHS_ALTOGETHER, SWATH_HEIGHT, 2, RASTER_BREADTH), ((0, 4), (1, 32)), -0.2, 0.2)), 0.0099487305, 1.0).astype(jnp.bfloat16)
    destination_patch_keys = jax.random.split(jax.random.fold_in(splits[1], 1), SWATHS_ALTOGETHER // SWATHS_HELD)
    destination_patch_turns = jax.random.permutation(jax.random.fold_in(splits[1], 3), SWATHS_ALTOGETHER // SWATHS_HELD)
    destination_patch = jax.vmap(lambda own, number: shared_out(jax.random.fold_in(splits[1], 2), own, number, SWATHS_HELD, N_TILE, 1, SHIPMENT_BOUND, 1))(destination_patch_keys, destination_patch_turns).reshape((SWATHS_ALTOGETHER, 1))
    swath_leading_scanline = touch_ends(jax.random.randint(splits[2], (SWATHS_ALTOGETHER,), 0, PATCH_HEIGHT - SWATH_HEIGHT + 1), jax.random.fold_in(splits[2], 1), 0, PATCH_HEIGHT - SWATH_HEIGHT).astype(jnp.int32)
    receiver_floor_intensity = jnp.clip(jnp.exp(math.log(1.0) - 2.3025851 * jax.random.uniform(splits[3], (PASSES_ALTOGETHER, N_TILE * PATCH_HEIGHT, 2, RASTER_BREADTH), jnp.float32) ** level_of(splits[3], (PASSES_ALTOGETHER, N_TILE * PATCH_HEIGHT, 2, RASTER_BREADTH), ((0, 4), (1, 32)), -0.2, 0.2)), 0.1, 1.0)
    return dict(swath_intensities=swath_intensities, destination_patch=destination_patch, swath_leading_scanline=swath_leading_scanline, receiver_floor_intensity=receiver_floor_intensity)


def box_mean(field, row_axis, col_axis):
    total = field
    scale = jnp.ones((), jnp.float32)
    for axis in (row_axis, col_axis):
        length = field.shape[axis]
        widths = [(0, 0)] * field.ndim
        widths[axis] = (3, 3)
        padded = jnp.pad(total, widths)
        summed = lax.slice_in_dim(padded, 0, length, axis=axis)
        for shift_by in range(1, 7):
            summed = summed + lax.slice_in_dim(padded, shift_by, shift_by + length, axis=axis)
        total = summed
        places = jnp.arange(length, dtype=jnp.int32)
        counted = (jnp.minimum(places + 3, length - 1) - jnp.maximum(places - 3, 0) + 1).astype(jnp.float32)
        view = [1] * field.ndim
        view[axis] = length
        scale = scale * counted.reshape(view)
    return total / scale


def reference(swath_intensities, destination_patch, swath_leading_scanline, receiver_floor_intensity):
    first_rows = (destination_patch[:, 0] * PATCH_HEIGHT + swath_leading_scanline).astype(jnp.int32)

    def insert_swath(swath_ordinal, raster_patch):
        leading_scanline = first_rows[swath_ordinal]
        single_swath = swath_intensities[:, swath_ordinal].astype(jnp.float32)
        running_patch = lax.dynamic_slice_in_dim(raster_patch, leading_scanline, SWATH_HEIGHT, 1)
        return lax.dynamic_update_slice_in_dim(raster_patch, running_patch + single_swath, leading_scanline, 1)

    raster_patch = lax.fori_loop(0, SWATHS_ALTOGETHER, insert_swath, receiver_floor_intensity.astype(jnp.float32))
    tiles = raster_patch.reshape(PASSES_ALTOGETHER, N_TILE, PATCH_HEIGHT, 2, RASTER_BREADTH)
    means = box_mean(tiles, 2, 4)
    ratio_sum = jnp.sum(tiles / means, axis=0) / PASSES_ALTOGETHER
    filtered = (means * ratio_sum).astype(jnp.bfloat16)
    return filtered.reshape(PASSES_ALTOGETHER, N_TILE * PATCH_HEIGHT, 2, RASTER_BREADTH)
```

```python
import functools

import jax
import jax.numpy as jnp
from jax import lax
from jax.experimental import pallas as pl
from jax.experimental.pallas import tpu as pltpu
from jax.sharding import PartitionSpec as P

MESH = pl.DeviceIdType.MESH
RING = 4
BOUNDS = (0, 32, 64, 96, 128)
LAG = 4
HALF = 3
GROUPS = (2, 1, 3, 0)
CHUNK = 16
FILTER_CHUNK = 4


def owner_of(first, second, core):
    x = first * (1 - core) + second * core
    z = second * (1 - core) + first * core
    return (x * RING + z) * 2 + core


def shift_columns(rows, by):
    lane = lax.broadcasted_iota(jnp.int32, rows.shape, 2)
    sub = lax.broadcasted_iota(jnp.int32, rows.shape, 1)
    turned = pltpu.roll(rows, by % 128, 2)
    if by > 0:
        beside = jnp.where(sub < 2, 0.0, pltpu.roll(turned, 2, 1))
        return jnp.where(lane < by, beside, turned)
    beside = jnp.where(sub >= 6, 0.0, pltpu.roll(turned, 6, 1))
    return jnp.where(lane >= 128 + by, beside, turned)


def kernel(
    blocks, block_rows, tile_rows, n_tile,
    swath, dest, lead, floor, out,
    raw, table, xs, xr, a1s, a1r, a2s, a2r, b2s, b2r, bs, br, canvas, means, own_ratio, ds_, dr,
    raw_sem, floor_sem, x_ss, x_rs, a1_ss, a1_rs, a2_ss, a2_rs, b2_ss, b2_rs, b_ss, b_rs, d_ss, d_rs,
):
    bf16, f32 = jnp.bfloat16, jnp.float32
    tile, date = lax.axis_index("tile"), lax.axis_index("date")
    core = tile % 2
    x, z = tile // (2 * RING), (tile // 2) % RING
    a = x * (1 - core) + z * core
    b = z * (1 - core) + x * core
    pieces = len(BOUNDS) - 1
    stride = tile_rows
    pad = stride - block_rows

    loads = [
        pltpu.make_async_copy(
            swath.at[pl.ds(i * block_rows, block_rows)],
            raw.at[pl.ds(i * stride + pad, block_rows)],
            raw_sem.at[i],
        )
        for i in range(blocks)
    ]
    for copy in loads:
        copy.start()
    floor_copy = pltpu.make_async_copy(floor, canvas.at[pl.ds(HALF, tile_rows)], floor_sem)
    floor_copy.start()

    partner = (date, owner_of(b, a, 1 - core))
    ahead = (date, owner_of((a + 1) % RING, b, core))
    behind = (date, owner_of((a + RING - 1) % RING, b, core))
    across = [(date, owner_of(a, (b + j) % RING, core)) for j in (1, 2, 3)]
    dates = [((date + j) % RING, tile) for j in (1, 2, 3)]
    barrier = pltpu.get_barrier_semaphore()
    everyone = [partner, ahead, behind] + across + dates
    for device in everyone:
        pl.semaphore_signal(barrier, inc=1, device_id=device, device_id_type=MESH)

    def clear(i, _):
        raw[pl.ds(i * stride, pad)] = jnp.zeros((pad, 8, 128), bf16)
        return 0

    lax.fori_loop(0, blocks, clear, 0)
    raw[pl.ds(blocks * stride, tile_rows)] = jnp.zeros((tile_rows, 8, 128), bf16)
    canvas[pl.ds(0, HALF)] = jnp.zeros((HALF, 8, 128), f32)
    canvas[pl.ds(HALF + tile_rows, HALF)] = jnp.zeros((HALF, 8, 128), f32)

    names = [dest[i] for i in range(blocks)]
    starts = [i * stride + pad - jnp.clip(lead[i], 0, pad) for i in range(blocks)]
    empty = blocks * stride

    def fill(o, _):
        least, second = jnp.int32(empty), jnp.int32(empty)
        for i in range(blocks):
            here = jnp.where(names[i] == o, starts[i], empty)
            second = jnp.minimum(second, jnp.maximum(least, here))
            least = jnp.minimum(least, here)
        table[2 * o] = least
        table[2 * o + 1] = second
        return 0

    lax.fori_loop(0, n_tile, fill, 0)

    for copy in loads:
        copy.wait()
    pl.semaphore_wait(barrier, len(everyone))

    sent = []

    def send(src, dst, ss, rs, device):
        copy = pltpu.make_async_remote_copy(
            src_ref=src, dst_ref=dst, send_sem=ss, recv_sem=rs, device_id=device, device_id_type=MESH
        )
        copy.start()
        sent.append(copy)
        return copy

    def spread(first, count, p, owner, store):
        low, high = BOUNDS[p], BOUNDS[p + 1]
        chunks = (high - low) // CHUNK

        def one(i, _):
            j = first + i // chunks
            row = low + (i % chunks) * CHUNK
            o = owner(j)
            one_, two_ = table[2 * o], table[2 * o + 1]
            total = raw[pl.ds(one_ + row, CHUNK)].astype(f32) + raw[pl.ds(two_ + row, CHUNK)].astype(f32)
            store(j, pl.ds(row, CHUNK), total)
            return 0

        lax.fori_loop(0, count * chunks, one, 0)

    x_copies, a1_copies, a2_copies, b2_copies, b_copies, d_copies = {}, {}, {}, {}, {}, {}

    def rows_of(p):
        return pl.ds(BOUNDS[p], BOUNDS[p + 1] - BOUNDS[p])

    def mine(step):
        return lambda j: owner_of((a + step) % RING, (b + j) % RING, core)

    def to_partner(p):
        for g, step in enumerate(GROUPS):

            def keep(j, rows, total):
                xs[g, j, rows] = total.astype(bf16)

            spread(0, RING, p, lambda j: owner_of((b + step) % RING, (a + j) % RING, 1 - core), keep)
            k = p * RING + g
            x_copies[p, g] = send(
                xs.at[g, :, rows_of(p)], xr.at[g, :, rows_of(p)], x_ss.at[k], x_rs.at[k], partner
            )

    def first_sends(p):
        x_copies[p, 0].wait_recv()

        def keep(j, rows, total):
            a1s[j, rows] = (total + xr[0, j, rows].astype(f32)).astype(bf16)

        spread(0, RING, p, mine(2), keep)
        for way, device in enumerate((ahead, behind)):
            k = p * 2 + way
            part = pl.ds(2 * way, 2)
            a1_copies[p, way] = send(
                a1s.at[part, rows_of(p)], a1r.at[part, rows_of(p)], a1_ss.at[k], a1_rs.at[k], device
            )
        for way, device in enumerate((ahead, behind)):
            g = 1 + way
            x_copies[p, g].wait_recv()

            def keep_far(j, rows, total):
                a2s[j, rows] = (total + xr[g, j, rows].astype(f32)).astype(bf16)

            spread(2 - 2 * way, 2, p, mine(GROUPS[g]), keep_far)
            k = p * 2 + way
            part = pl.ds(2 - 2 * way, 2)
            a2_copies[p, way] = send(
                a2s.at[part, rows_of(p)], a2r.at[part, rows_of(p)], a2_ss.at[k], a2_rs.at[k], device
            )

    def second_sends(p):
        for way, device in enumerate((ahead, behind)):
            g = 1 + way
            a1_copies[p, way].wait_recv()

            def keep(j, rows, total):
                total = total + xr[g, j, rows].astype(f32) + a1r[j, rows].astype(f32)
                b2s[j, rows] = total.astype(bf16)

            spread(2 * way, 2, p, mine(GROUPS[g]), keep)
            k = p * 2 + way
            part = pl.ds(2 * way, 2)
            b2_copies[p, way] = send(
                b2s.at[part, rows_of(p)], b2r.at[part, rows_of(p)], b2_ss.at[k], b2_rs.at[k], device
            )

    def cross(p):
        x_copies[p, 3].wait_recv()
        for way in range(2):
            a2_copies[p, way].wait_recv()
            b2_copies[p, way].wait_recv()

        def summed(j, rows, total):
            total = total + xr[3, j, rows].astype(f32)
            return total + a2r[j, rows].astype(f32) + b2r[j, rows].astype(f32)

        def keep(j, rows, total):
            bs[j - 1, rows] = summed(j, rows, total).astype(bf16)

        def keep_own(j, rows, total):
            here = pl.ds(HALF + rows.start, CHUNK)
            canvas[here] += summed(0, rows, total)

        spread(1, RING - 1, p, mine(0), keep)
        for j in (2, 1, 3):
            k = p * 3 + j - 1
            b_copies[p, j] = send(
                bs.at[j - 1, rows_of(p)], br.at[j - 1, rows_of(p)], b_ss.at[k], b_rs.at[k], across[j - 1]
            )
        if p == 0:
            floor_copy.wait()
        spread(0, 1, p, mine(0), keep_own)

    def filtered_rows(p):
        low = max(0, BOUNDS[p] - LAG)
        high = tile_rows if p == pieces - 1 else BOUNDS[p + 1] - LAG
        return low, high

    def box(p):
        for j in (1, 2, 3):
            b_copies[p, j].wait_recv()
        low, high = BOUNDS[p], BOUNDS[p + 1]

        def add(i, _):
            row = low + i * CHUNK
            rows = pl.ds(row, CHUNK)
            canvas[pl.ds(HALF + row, CHUNK)] += (
                br[0, rows].astype(f32) + br[1, rows].astype(f32) + br[2, rows].astype(f32)
            )
            return 0

        lax.fori_loop(0, (high - low) // CHUNK, add, 0)
        low, high = filtered_rows(p)
        shape = (FILTER_CHUNK, 8, 128)
        column = (lax.broadcasted_iota(jnp.int32, shape, 1) // 2) * 128 + lax.broadcasted_iota(jnp.int32, shape, 2)
        last = 4 * 128 - 1
        wide = jnp.minimum(column + HALF, last) - jnp.maximum(column - HALF, 0) + 1
        wide = wide.astype(f32)

        def smooth(i, _):
            row = low + i * FILTER_CHUNK
            total = canvas[pl.ds(row, FILTER_CHUNK)]
            for k in range(1, 2 * HALF + 1):
                total = total + canvas[pl.ds(row + k, FILTER_CHUNK)]
            summed = total
            for k in range(1, HALF + 1):
                summed = summed + (shift_columns(total, k) + shift_columns(total, -k))
            at = row + lax.broadcasted_iota(jnp.int32, shape, 0)
            tall = jnp.minimum(at + HALF, tile_rows - 1) - jnp.maximum(at - HALF, 0) + 1
            mean = summed / (tall.astype(f32) * wide)
            ratio = canvas[pl.ds(row + HALF, FILTER_CHUNK)] / mean
            rows = pl.ds(row, FILTER_CHUNK)
            means[rows] = mean
            own_ratio[rows] = ratio
            ds_[rows] = ratio.astype(bf16)
            return 0

        lax.fori_loop(0, (high - low) // FILTER_CHUNK, smooth, 0)
        rows = pl.ds(low, high - low)
        for j in (2, 1, 3):
            k = p * 3 + j - 1
            d_copies[p, j] = send(ds_.at[rows], dr.at[j - 1, rows], d_ss.at[k], d_rs.at[k], dates[j - 1])

    def finish(p):
        for j in (1, 2, 3):
            d_copies[p, j].wait_recv()
        low, high = filtered_rows(p)

        def one(i, _):
            rows = pl.ds(low + i * FILTER_CHUNK, FILTER_CHUNK)
            total = own_ratio[rows] + dr[0, rows].astype(f32)
            total = total + (dr[1, rows].astype(f32) + dr[2, rows].astype(f32))
            out[rows] = (means[rows] * (total * (1.0 / RING))).astype(bf16)
            return 0

        lax.fori_loop(0, (high - low) // FILTER_CHUNK, one, 0)

    stages = (to_partner, first_sends, second_sends, cross, box, finish)
    for t in range(pieces + len(stages) - 1):
        for s, stage in enumerate(stages):
            if 0 <= t - s < pieces:
                stage(t - s)
    for copy in sent:
        copy.wait_send()


def per_device(swath_intensities, destination_patch, swath_leading_scanline, receiver_floor_intensity):
    _, blocks, block_rows, pols, width = swath_intensities.shape
    tile_rows = receiver_floor_intensity.shape[1]
    n_tile = lax.axis_size("tile")
    cols = width // 128

    def rowwise(array, rows):
        return array.reshape(rows, pols, cols, 128).transpose(0, 2, 1, 3).reshape(rows, pols * cols, 128)

    pieces = len(BOUNDS) - 1
    bf16, f32 = jnp.bfloat16, jnp.float32

    def buffer(*lead, dtype=bf16):
        return pltpu.VMEM((*lead, 8, 128), dtype)

    dma = pltpu.SemaphoreType.DMA
    scratch = [
        buffer(blocks * tile_rows + tile_rows),
        pltpu.SMEM((2 * n_tile,), jnp.int32),
        buffer(4, 4, tile_rows), buffer(4, 4, tile_rows),
        buffer(4, tile_rows), buffer(4, tile_rows),
        buffer(4, tile_rows), buffer(4, tile_rows),
        buffer(4, tile_rows), buffer(4, tile_rows),
        buffer(3, tile_rows), buffer(3, tile_rows),
        buffer(tile_rows + 2 * HALF, dtype=f32),
        buffer(tile_rows, dtype=f32), buffer(tile_rows, dtype=f32),
        buffer(tile_rows), buffer(3, tile_rows),
        dma((blocks,)), dma,
        dma((pieces * 4,)), dma((pieces * 4,)),
        dma((pieces * 2,)), dma((pieces * 2,)),
        dma((pieces * 2,)), dma((pieces * 2,)),
        dma((pieces * 2,)), dma((pieces * 2,)),
        dma((pieces * 3,)), dma((pieces * 3,)),
        dma((pieces * 3,)), dma((pieces * 3,)),
    ]
    filtered = pl.pallas_call(
        functools.partial(kernel, blocks, block_rows, tile_rows, n_tile),
        out_shape=jax.ShapeDtypeStruct((tile_rows, pols * cols, 128), bf16),
        in_specs=[
            pl.BlockSpec(memory_space=pl.ANY),
            pl.BlockSpec(memory_space=pltpu.SMEM),
            pl.BlockSpec(memory_space=pltpu.SMEM),
            pl.BlockSpec(memory_space=pl.ANY),
        ],
        out_specs=pl.BlockSpec(memory_space=pltpu.VMEM),
        scratch_shapes=scratch,
        compiler_params=pltpu.CompilerParams(
            collective_id=0, has_side_effects=True, vmem_limit_bytes=60 << 20
        ),
        name="quegan",
    )(
        rowwise(swath_intensities, blocks * block_rows),
        destination_patch[:, 0],
        swath_leading_scanline,
        rowwise(receiver_floor_intensity, tile_rows),
    )
    return filtered.reshape(tile_rows, cols, pols, 128).transpose(0, 2, 1, 3).reshape(1, tile_rows, pols, width)


def solution(mesh):
    return jax.shard_map(
        per_device,
        mesh=mesh,
        in_specs=(
            P("date", "tile", None, None, None),
            P("tile", None),
            P("tile"),
            P("date", "tile", None, None),
        ),
        out_specs=P("date", "tile", None, None),
        check_vma=False,
    )
```

```python
import functools

import jax
import jax.numpy as jnp
from jax import lax
from jax.experimental import pallas as pl
from jax.experimental.pallas import tpu as pltpu
from jax.sharding import PartitionSpec as P

MESH = pl.DeviceIdType.MESH
RING = 4
BOUNDS = (0, 16, 32, 48, 64, 80, 96, 112, 128)
LAGS = (0, 1, 4, 7, 9.5, 20)
FIRST = True
LAG = 4
HALF = 3
GROUPS = (2, 1, 3, 0)
CHUNK = 16
FILTER_CHUNK = 4


def owner_of(first, second, core):
    x = first * (1 - core) + second * core
    z = second * (1 - core) + first * core
    return (x * RING + z) * 2 + core


def shift_columns(rows, by):
    lane = lax.broadcasted_iota(jnp.int32, rows.shape, 2)
    sub = lax.broadcasted_iota(jnp.int32, rows.shape, 1)
    turned = pltpu.roll(rows, by % 128, 2)
    if by > 0:
        beside = jnp.where(sub < 2, 0.0, pltpu.roll(turned, 2, 1))
        return jnp.where(lane < by, beside, turned)
    beside = jnp.where(sub >= 6, 0.0, pltpu.roll(turned, 6, 1))
    return jnp.where(lane >= 128 + by, beside, turned)


def kernel(
    blocks, block_rows, tile_rows, n_tile,
    swath, dest, lead, floor, out,
    raw, windows, table, xs, xr, as_, ar, b2s, b2r, bs, br, canvas, means, own_ratio, ds_, dr,
    raw_sem, table_sem, floor_sem, x_ss, x_rs, a_ss, a_rs, b2_ss, b2_rs, b_ss, b_rs, d_ss, d_rs,
):
    bf16, f32 = jnp.bfloat16, jnp.float32
    tile, date = lax.axis_index("tile"), lax.axis_index("date")
    core = tile % 2
    x, z = tile // (2 * RING), (tile // 2) % RING
    a = x * (1 - core) + z * core
    b = z * (1 - core) + x * core
    pieces = len(BOUNDS) - 1
    stride = tile_rows
    pad = stride - block_rows

    partner = (date, owner_of(b, a, 1 - core))
    ahead = (date, owner_of((a + 1) % RING, b, core))
    behind = (date, owner_of((a + RING - 1) % RING, b, core))
    across = [(date, owner_of(a, (b + j) % RING, core)) for j in (1, 2, 3)]
    dates = [((date + j) % RING, tile) for j in (1, 2, 3)]
    barrier = pltpu.get_barrier_semaphore()
    everyone = [partner, ahead, behind] + across + dates
    for device in everyone:
        pl.semaphore_signal(barrier, inc=1, device_id=device, device_id_type=MESH)

    loads = [
        pltpu.make_async_copy(
            swath.at[pl.ds(i * block_rows, block_rows)],
            raw.at[pl.ds(i * stride + pad, block_rows)],
            raw_sem.at[i],
        )
        for i in range(blocks)
    ]
    for copy in loads:
        copy.start()
    floor_copy = pltpu.make_async_copy(floor, canvas.at[pl.ds(HALF, tile_rows)], floor_sem)
    floor_copy.start()

    names = [dest[i] for i in range(blocks)]
    starts = [i * stride + pad - jnp.clip(lead[i], 0, pad) for i in range(blocks)]
    empty = blocks * stride

    owner = lax.broadcasted_iota(jnp.int32, (8, 128), 1)
    least = jnp.full((8, 128), empty, jnp.int32)
    other = least
    for i in range(blocks):
        here = jnp.where(owner == names[i], starts[i], empty)
        other = jnp.minimum(other, jnp.maximum(least, here))
        least = jnp.minimum(least, here)
    windows[0] = least
    windows[1] = other
    table_copy = pltpu.make_async_copy(windows, table, table_sem)
    table_copy.start()

    def clear(i, _):
        raw[pl.ds(i * stride, pad)] = jnp.zeros((pad, 8, 128), bf16)
        return 0

    lax.fori_loop(0, blocks, clear, 0)
    raw[pl.ds(blocks * stride, tile_rows)] = jnp.zeros((tile_rows, 8, 128), bf16)
    canvas[pl.ds(0, HALF)] = jnp.zeros((HALF, 8, 128), f32)
    canvas[pl.ds(HALF + tile_rows, HALF)] = jnp.zeros((HALF, 8, 128), f32)

    table_copy.wait()
    for copy in loads:
        copy.wait()
    pl.semaphore_wait(barrier, len(everyone))

    sent = []

    def send(src, dst, ss, rs, device):
        copy = pltpu.make_async_remote_copy(
            src_ref=src, dst_ref=dst, send_sem=ss, recv_sem=rs, device_id=device, device_id_type=MESH
        )
        copy.start()
        sent.append(copy)
        return copy

    def spread(first, count, p, owner, store):
        low, high = BOUNDS[p], BOUNDS[p + 1]
        chunks = (high - low) // CHUNK

        def one(i, _):
            j = first + i // chunks
            row = low + (i % chunks) * CHUNK
            o = owner(j)
            one_, two_ = table[0, 0, o], table[1, 0, o]
            total = raw[pl.ds(one_ + row, CHUNK)].astype(f32) + raw[pl.ds(two_ + row, CHUNK)].astype(f32)
            store(j, pl.ds(row, CHUNK), total)
            return 0

        lax.fori_loop(0, count * chunks, one, 0)

    x_copies, a_copies, b2_copies, b_copies, d_copies = {}, {}, {}, {}, {}

    def rows_of(p):
        return pl.ds(BOUNDS[p], BOUNDS[p + 1] - BOUNDS[p])

    def mine(step):
        return lambda j: owner_of((a + step) % RING, (b + j) % RING, core)

    def to_partner(p):
        for k, groups in enumerate(((0, 1, 2), (3,))):
            for g in groups:

                def keep(j, rows, total):
                    xs[g, j, rows] = total.astype(bf16)

                step = GROUPS[g]
                spread(0, RING, p, lambda j: owner_of((b + step) % RING, (a + j) % RING, 1 - core), keep)
            part, n = pl.ds(groups[0], len(groups)), p * 2 + k
            x_copies[p, k] = send(
                xs.at[part, :, rows_of(p)], xr.at[part, :, rows_of(p)], x_ss.at[n], x_rs.at[n], partner
            )

    def first_sends(p):
        x_copies[p, 0].wait_recv()
        for way, device in enumerate((ahead, behind)):
            for g, first in ((0, 2 * way), (1 + way, 2 - 2 * way)):

                def keep(j, rows, total):
                    as_[way, j, rows] = (total + xr[g, j, rows].astype(f32)).astype(bf16)

                spread(first, 2, p, mine(GROUPS[g]), keep)
            k = p * 2 + way
            a_copies[p, way] = send(
                as_.at[way, :, rows_of(p)], ar.at[way, :, rows_of(p)], a_ss.at[k], a_rs.at[k], device
            )

    def second_sends(p):
        for way, device in enumerate((ahead, behind)):
            g = 1 + way
            a_copies[p, way].wait_recv()

            def keep(j, rows, total):
                total = total + xr[g, j, rows].astype(f32) + ar[way, j, rows].astype(f32)
                b2s[j, rows] = total.astype(bf16)

            spread(2 * way, 2, p, mine(GROUPS[g]), keep)
            k = p * 2 + way
            part = pl.ds(2 * way, 2)
            b2_copies[p, way] = send(
                b2s.at[part, rows_of(p)], b2r.at[part, rows_of(p)], b2_ss.at[k], b2_rs.at[k], device
            )

    def cross(p):
        x_copies[p, 1].wait_recv()
        for way in range(2):
            b2_copies[p, way].wait_recv()

        def summed(j, rows, total):
            total = total + xr[3, j, rows].astype(f32)
            return total + ar[1 - j // 2, j, rows].astype(f32) + b2r[j, rows].astype(f32)

        def keep(j, rows, total):
            bs[j - 1, rows] = summed(j, rows, total).astype(bf16)

        def keep_own(j, rows, total):
            here = pl.ds(HALF + rows.start, CHUNK)
            canvas[here] += summed(0, rows, total)

        spread(1, RING - 1, p, mine(0), keep)
        for j in (2, 1, 3):
            k = p * 3 + j - 1
            b_copies[p, j] = send(
                bs.at[j - 1, rows_of(p)], br.at[j - 1, rows_of(p)], b_ss.at[k], b_rs.at[k], across[j - 1]
            )
        if p == 0:
            floor_copy.wait()
        spread(0, 1, p, mine(0), keep_own)

    def filtered_rows(p):
        low = max(0, BOUNDS[p] - LAG)
        high = tile_rows if p == pieces - 1 else BOUNDS[p + 1] - LAG
        return low, high

    def box(p):
        for j in (1, 2, 3):
            b_copies[p, j].wait_recv()
        low, high = BOUNDS[p], BOUNDS[p + 1]

        def add(i, _):
            row = low + i * CHUNK
            rows = pl.ds(row, CHUNK)
            canvas[pl.ds(HALF + row, CHUNK)] += (
                br[0, rows].astype(f32) + br[1, rows].astype(f32) + br[2, rows].astype(f32)
            )
            return 0

        lax.fori_loop(0, (high - low) // CHUNK, add, 0)
        low, high = filtered_rows(p)
        shape = (FILTER_CHUNK, 8, 128)
        column = (lax.broadcasted_iota(jnp.int32, shape, 1) // 2) * 128 + lax.broadcasted_iota(jnp.int32, shape, 2)
        last = 4 * 128 - 1
        wide = jnp.minimum(column + HALF, last) - jnp.maximum(column - HALF, 0) + 1
        wide = wide.astype(f32)

        def smooth(i, _):
            row = low + i * FILTER_CHUNK
            total = canvas[pl.ds(row, FILTER_CHUNK)]
            for k in range(1, 2 * HALF + 1):
                total = total + canvas[pl.ds(row + k, FILTER_CHUNK)]
            summed = total
            for k in range(1, HALF + 1):
                summed = summed + (shift_columns(total, k) + shift_columns(total, -k))
            at = row + lax.broadcasted_iota(jnp.int32, shape, 0)
            tall = jnp.minimum(at + HALF, tile_rows - 1) - jnp.maximum(at - HALF, 0) + 1
            mean = summed / (tall.astype(f32) * wide)
            ratio = canvas[pl.ds(row + HALF, FILTER_CHUNK)] / mean
            rows = pl.ds(row, FILTER_CHUNK)
            means[rows] = mean
            own_ratio[rows] = ratio
            ds_[rows] = ratio.astype(bf16)
            return 0

        lax.fori_loop(0, (high - low) // FILTER_CHUNK, smooth, 0)
        rows = pl.ds(low, high - low)
        for j in (2, 1, 3):
            k = p * 3 + j - 1
            d_copies[p, j] = send(ds_.at[rows], dr.at[j - 1, rows], d_ss.at[k], d_rs.at[k], dates[j - 1])

    def finish(p):
        for j in (1, 2, 3):
            d_copies[p, j].wait_recv()
        low, high = filtered_rows(p)

        def one(i, _):
            rows = pl.ds(low + i * FILTER_CHUNK, FILTER_CHUNK)
            total = own_ratio[rows] + dr[0, rows].astype(f32)
            total = total + (dr[1, rows].astype(f32) + dr[2, rows].astype(f32))
            out[rows] = (means[rows] * (total * (1.0 / RING))).astype(bf16)
            return 0

        lax.fori_loop(0, (high - low) // FILTER_CHUNK, one, 0)

    stages = (to_partner, first_sends, second_sends, cross, box, finish)
    steps = [(p + LAGS[s], (s if FIRST else -s), p, s) for p in range(pieces) for s in range(len(stages))]
    for _, _, p, s in sorted(steps):
        stages[s](p)
    for copy in sent:
        copy.wait_send()


def per_device(swath_intensities, destination_patch, swath_leading_scanline, receiver_floor_intensity):
    _, blocks, block_rows, pols, width = swath_intensities.shape
    tile_rows = receiver_floor_intensity.shape[1]
    n_tile = lax.axis_size("tile")
    cols = width // 128

    def rowwise(array, rows):
        return array.reshape(rows, pols, cols, 128).transpose(0, 2, 1, 3).reshape(rows, pols * cols, 128)

    pieces = len(BOUNDS) - 1
    bf16, f32 = jnp.bfloat16, jnp.float32

    def buffer(*lead, dtype=bf16):
        return pltpu.VMEM((*lead, 8, 128), dtype)

    dma = pltpu.SemaphoreType.DMA
    scratch = [
        buffer(blocks * tile_rows + tile_rows),
        pltpu.VMEM((2, 8, 128), jnp.int32), pltpu.SMEM((2, 8, 128), jnp.int32),
        buffer(4, 4, tile_rows), buffer(4, 4, tile_rows),
        buffer(2, 4, tile_rows), buffer(2, 4, tile_rows),
        buffer(4, tile_rows), buffer(4, tile_rows),
        buffer(3, tile_rows), buffer(3, tile_rows),
        buffer(tile_rows + 2 * HALF, dtype=f32),
        buffer(tile_rows, dtype=f32), buffer(tile_rows, dtype=f32),
        buffer(tile_rows), buffer(3, tile_rows),
        dma((blocks,)), dma, dma,
        dma((pieces * 2,)), dma((pieces * 2,)),
        dma((pieces * 2,)), dma((pieces * 2,)),
        dma((pieces * 2,)), dma((pieces * 2,)),
        dma((pieces * 3,)), dma((pieces * 3,)),
        dma((pieces * 3,)), dma((pieces * 3,)),
    ]
    filtered = pl.pallas_call(
        functools.partial(kernel, blocks, block_rows, tile_rows, n_tile),
        out_shape=jax.ShapeDtypeStruct((tile_rows, pols * cols, 128), bf16),
        in_specs=[
            pl.BlockSpec(memory_space=pl.ANY),
            pl.BlockSpec(memory_space=pltpu.SMEM),
            pl.BlockSpec(memory_space=pltpu.SMEM),
            pl.BlockSpec(memory_space=pl.ANY),
        ],
        out_specs=pl.BlockSpec(memory_space=pltpu.VMEM),
        scratch_shapes=scratch,
        compiler_params=pltpu.CompilerParams(
            collective_id=0, has_side_effects=True, vmem_limit_bytes=60 << 20
        ),
        name="quegan",
    )(
        rowwise(swath_intensities, blocks * block_rows),
        destination_patch[:, 0],
        swath_leading_scanline,
        rowwise(receiver_floor_intensity, tile_rows),
    )
    return filtered.reshape(tile_rows, cols, pols, 128).transpose(0, 2, 1, 3).reshape(1, tile_rows, pols, width)


def solution(mesh):
    return jax.shard_map(
        per_device,
        mesh=mesh,
        in_specs=(
            P("date", "tile", None, None, None),
            P("tile", None),
            P("tile"),
            P("date", "tile", None, None),
        ),
        out_specs=P("date", "tile", None, None),
        check_vma=False,
    )
```

```python
import functools

import jax
import jax.numpy as jnp
from jax import lax
from jax.experimental import pallas as pl
from jax.experimental.pallas import tpu as pltpu
from jax.sharding import PartitionSpec as P

MESH = pl.DeviceIdType.MESH
RING = 4
BOUNDS = (0, 8, 24, 40, 56, 72, 88, 104, 120, 128)
LAGS = (0, 16, 64, 112, 152, 400)
LAG = 8
HALF = 3
GROUPS = (2, 1, 3, 0)
CHUNK = 16
FILTER_CHUNK = 8


def owner_of(first, second, core):
    x = first * (1 - core) + second * core
    z = second * (1 - core) + first * core
    return (x * RING + z) * 2 + core


def shift_columns(rows, by):
    lane = lax.broadcasted_iota(jnp.int32, rows.shape, 2)
    sub = lax.broadcasted_iota(jnp.int32, rows.shape, 1)
    turned = pltpu.roll(rows, by % 128, 2)
    if by > 0:
        beside = jnp.where(sub < 2, 0.0, pltpu.roll(turned, 2, 1))
        return jnp.where(lane < by, beside, turned)
    beside = jnp.where(sub >= 6, 0.0, pltpu.roll(turned, 6, 1))
    return jnp.where(lane >= 128 + by, beside, turned)


def kernel(
    blocks, block_rows, tile_rows, n_tile,
    swath, dest, lead, floor, out,
    raw, windows, table, xs, xr, as_, ar, b2s, b2r, bs, br, canvas, means, own_ratio, ds_, dr,
    raw_sem, table_sem, floor_sem, x_ss, x_rs, a_ss, a_rs, b2_ss, b2_rs, b_ss, b_rs, d_ss, d_rs,
):
    bf16, f32 = jnp.bfloat16, jnp.float32
    tile, date = lax.axis_index("tile"), lax.axis_index("date")
    core = tile % 2
    x, z = tile // (2 * RING), (tile // 2) % RING
    a = x * (1 - core) + z * core
    b = z * (1 - core) + x * core
    pieces = len(BOUNDS) - 1
    stride = tile_rows
    pad = stride - block_rows

    partner = (date, owner_of(b, a, 1 - core))
    ahead = (date, owner_of((a + 1) % RING, b, core))
    behind = (date, owner_of((a + RING - 1) % RING, b, core))
    across = [(date, owner_of(a, (b + j) % RING, core)) for j in (1, 2, 3)]
    dates = [((date + j) % RING, tile) for j in (1, 2, 3)]
    barrier = pltpu.get_barrier_semaphore()
    everyone = [partner, ahead, behind] + across + dates
    for device in everyone:
        pl.semaphore_signal(barrier, inc=1, device_id=device, device_id_type=MESH)

    loads = [
        pltpu.make_async_copy(
            swath.at[pl.ds(i * block_rows, block_rows)],
            raw.at[pl.ds(i * stride + pad, block_rows)],
            raw_sem.at[i],
        )
        for i in range(blocks)
    ]
    for copy in loads:
        copy.start()
    floor_copy = pltpu.make_async_copy(floor, canvas.at[pl.ds(HALF, tile_rows)], floor_sem)
    floor_copy.start()

    names = [dest[i] for i in range(blocks)]
    starts = [i * stride + pad - jnp.clip(lead[i], 0, pad) for i in range(blocks)]
    empty = blocks * stride

    owner = lax.broadcasted_iota(jnp.int32, (8, 128), 1)
    least = jnp.full((8, 128), empty, jnp.int32)
    other = least
    for i in range(blocks):
        here = jnp.where(owner == names[i], starts[i], empty)
        other = jnp.minimum(other, jnp.maximum(least, here))
        least = jnp.minimum(least, here)
    windows[0] = least
    windows[1] = other
    table_copy = pltpu.make_async_copy(windows, table, table_sem)
    table_copy.start()

    def clear(i, _):
        raw[pl.ds(i * stride, pad)] = jnp.zeros((pad, 8, 128), bf16)
        return 0

    lax.fori_loop(0, blocks, clear, 0)
    raw[pl.ds(blocks * stride, tile_rows)] = jnp.zeros((tile_rows, 8, 128), bf16)
    canvas[pl.ds(0, HALF)] = jnp.zeros((HALF, 8, 128), f32)
    canvas[pl.ds(HALF + tile_rows, HALF)] = jnp.zeros((HALF, 8, 128), f32)

    table_copy.wait()
    for copy in loads:
        copy.wait()
    pl.semaphore_wait(barrier, len(everyone))

    sent = []

    def send(src, dst, ss, rs, device):
        copy = pltpu.make_async_remote_copy(
            src_ref=src, dst_ref=dst, send_sem=ss, recv_sem=rs, device_id=device, device_id_type=MESH
        )
        copy.start()
        sent.append(copy)
        return copy

    def spread(first, count, p, owner, store):
        low, high = BOUNDS[p], BOUNDS[p + 1]
        chunk = min(CHUNK, high - low)
        chunks = (high - low) // chunk

        def one(i, _):
            j = first + i // chunks
            row = low + (i % chunks) * chunk
            o = owner(j)
            one_, two_ = table[0, 0, o], table[1, 0, o]
            total = raw[pl.ds(one_ + row, chunk)] + raw[pl.ds(two_ + row, chunk)]
            store(j, pl.ds(row, chunk), total)
            return 0

        lax.fori_loop(0, count * chunks, one, 0)

    x_copies, a_copies, b2_copies, b_copies, d_copies = {}, {}, {}, {}, {}

    def rows_of(p):
        return pl.ds(BOUNDS[p], BOUNDS[p + 1] - BOUNDS[p])

    def mine(step):
        return lambda j: owner_of((a + step) % RING, (b + j) % RING, core)

    def to_partner(p):
        for k, groups in enumerate(((0, 1, 2), (3,))):
            for g in groups:

                def keep(j, rows, total):
                    xs[g, j, rows] = total

                step = GROUPS[g]
                spread(0, RING, p, lambda j: owner_of((b + step) % RING, (a + j) % RING, 1 - core), keep)
            part, n = pl.ds(groups[0], len(groups)), p * 2 + k
            x_copies[p, k] = send(
                xs.at[part, :, rows_of(p)], xr.at[part, :, rows_of(p)], x_ss.at[n], x_rs.at[n], partner
            )

    def first_sends(p):
        x_copies[p, 0].wait_recv()
        for way, device in enumerate((ahead, behind)):
            for g, first in ((0, 2 * way), (1 + way, 2 - 2 * way)):

                def keep(j, rows, total):
                    as_[way, j, rows] = total + xr[g, j, rows]

                spread(first, 2, p, mine(GROUPS[g]), keep)
            k = p * 2 + way
            a_copies[p, way] = send(
                as_.at[way, :, rows_of(p)], ar.at[way, :, rows_of(p)], a_ss.at[k], a_rs.at[k], device
            )

    def second_sends(p):
        for way, device in enumerate((ahead, behind)):
            g = 1 + way
            a_copies[p, way].wait_recv()

            def keep(j, rows, total):
                b2s[j, rows] = (total + xr[g, j, rows]) + ar[way, j, rows]

            spread(2 * way, 2, p, mine(GROUPS[g]), keep)
            k = p * 2 + way
            part = pl.ds(2 * way, 2)
            b2_copies[p, way] = send(
                b2s.at[part, rows_of(p)], b2r.at[part, rows_of(p)], b2_ss.at[k], b2_rs.at[k], device
            )

    def cross(p):
        x_copies[p, 1].wait_recv()
        for way in range(2):
            b2_copies[p, way].wait_recv()

        def summed(j, rows, total):
            total = total.astype(f32) + xr[3, j, rows].astype(f32)
            return total + ar[1 - j // 2, j, rows].astype(f32) + b2r[j, rows].astype(f32)

        def keep(j, rows, total):
            bs[j - 1, rows] = summed(j, rows, total).astype(bf16)

        def keep_own(j, rows, total):
            here = pl.ds(HALF + rows.start, rows.size)
            canvas[here] += summed(0, rows, total)

        spread(1, RING - 1, p, mine(0), keep)
        for j in (2, 1, 3):
            k = p * 3 + j - 1
            b_copies[p, j] = send(
                bs.at[j - 1, rows_of(p)], br.at[j - 1, rows_of(p)], b_ss.at[k], b_rs.at[k], across[j - 1]
            )
        if p == 0:
            floor_copy.wait()
        spread(0, 1, p, mine(0), keep_own)

    def filtered_rows(p):
        low = max(0, BOUNDS[p] - LAG)
        high = tile_rows if p == pieces - 1 else BOUNDS[p + 1] - LAG
        return low, high

    def box(p):
        for j in (1, 2, 3):
            b_copies[p, j].wait_recv()
        low, high = BOUNDS[p], BOUNDS[p + 1]

        def add(i, _):
            row = low + i * step
            rows = pl.ds(row, step)
            canvas[pl.ds(HALF + row, step)] += (
                br[0, rows].astype(f32) + br[1, rows].astype(f32) + br[2, rows].astype(f32)
            )
            return 0

        step = min(CHUNK, high - low)
        lax.fori_loop(0, (high - low) // step, add, 0)
        low, high = filtered_rows(p)
        shape = (FILTER_CHUNK, 8, 128)
        column = (lax.broadcasted_iota(jnp.int32, shape, 1) // 2) * 128 + lax.broadcasted_iota(jnp.int32, shape, 2)
        last = 4 * 128 - 1
        wide = jnp.minimum(column + HALF, last) - jnp.maximum(column - HALF, 0) + 1
        wide = wide.astype(f32)

        def smooth(i, _):
            row = low + i * FILTER_CHUNK
            total = canvas[pl.ds(row, FILTER_CHUNK)]
            for k in range(1, 2 * HALF + 1):
                total = total + canvas[pl.ds(row + k, FILTER_CHUNK)]
            summed = total
            for k in range(1, HALF + 1):
                summed = summed + (shift_columns(total, k) + shift_columns(total, -k))
            at = row + lax.broadcasted_iota(jnp.int32, shape, 0)
            tall = jnp.minimum(at + HALF, tile_rows - 1) - jnp.maximum(at - HALF, 0) + 1
            mean = summed / (tall.astype(f32) * wide)
            ratio = canvas[pl.ds(row + HALF, FILTER_CHUNK)] / mean
            rows = pl.ds(row, FILTER_CHUNK)
            means[rows] = mean
            own_ratio[rows] = ratio
            ds_[rows] = ratio.astype(bf16)
            return 0

        lax.fori_loop(0, (high - low) // FILTER_CHUNK, smooth, 0)
        rows = pl.ds(low, high - low)
        for j in (2, 1, 3):
            k = p * 3 + j - 1
            d_copies[p, j] = send(ds_.at[rows], dr.at[j - 1, rows], d_ss.at[k], d_rs.at[k], dates[j - 1])

    def finish(p):
        for j in (1, 2, 3):
            d_copies[p, j].wait_recv()
        low, high = filtered_rows(p)

        def one(i, _):
            rows = pl.ds(low + i * FILTER_CHUNK, FILTER_CHUNK)
            total = own_ratio[rows] + dr[0, rows].astype(f32)
            total = total + (dr[1, rows].astype(f32) + dr[2, rows].astype(f32))
            out[rows] = (means[rows] * (total * (1.0 / RING))).astype(bf16)
            return 0

        lax.fori_loop(0, (high - low) // FILTER_CHUNK, one, 0)

    stages = (to_partner, first_sends, second_sends, cross, box, finish)
    steps = [(BOUNDS[p + 1] + LAGS[s], s, p) for p in range(pieces) for s in range(len(stages))]
    steps.sort()
    for _, s, p in steps[:-1]:
        stages[s](p)
    for copy in sent[:-3]:
        copy.wait_send()
    finish(pieces - 1)
    for copy in sent[-3:]:
        copy.wait_send()


def per_device(swath_intensities, destination_patch, swath_leading_scanline, receiver_floor_intensity):
    _, blocks, block_rows, pols, width = swath_intensities.shape
    tile_rows = receiver_floor_intensity.shape[1]
    n_tile = lax.axis_size("tile")
    cols = width // 128

    def rowwise(array, rows):
        return array.reshape(rows, pols, cols, 128).transpose(0, 2, 1, 3).reshape(rows, pols * cols, 128)

    pieces = len(BOUNDS) - 1
    bf16, f32 = jnp.bfloat16, jnp.float32

    def buffer(*lead, dtype=bf16):
        return pltpu.VMEM((*lead, 8, 128), dtype)

    dma = pltpu.SemaphoreType.DMA
    scratch = [
        buffer(blocks * tile_rows + tile_rows),
        pltpu.VMEM((2, 8, 128), jnp.int32), pltpu.SMEM((2, 8, 128), jnp.int32),
        buffer(4, 4, tile_rows), buffer(4, 4, tile_rows),
        buffer(2, 4, tile_rows), buffer(2, 4, tile_rows),
        buffer(4, tile_rows), buffer(4, tile_rows),
        buffer(3, tile_rows), buffer(3, tile_rows),
        buffer(tile_rows + 2 * HALF, dtype=f32),
        buffer(tile_rows, dtype=f32), buffer(tile_rows, dtype=f32),
        buffer(tile_rows), buffer(3, tile_rows),
        dma((blocks,)), dma, dma,
        dma((pieces * 2,)), dma((pieces * 2,)),
        dma((pieces * 2,)), dma((pieces * 2,)),
        dma((pieces * 2,)), dma((pieces * 2,)),
        dma((pieces * 3,)), dma((pieces * 3,)),
        dma((pieces * 3,)), dma((pieces * 3,)),
    ]
    filtered = pl.pallas_call(
        functools.partial(kernel, blocks, block_rows, tile_rows, n_tile),
        out_shape=jax.ShapeDtypeStruct((tile_rows, pols * cols, 128), bf16),
        in_specs=[
            pl.BlockSpec(memory_space=pl.ANY),
            pl.BlockSpec(memory_space=pltpu.SMEM),
            pl.BlockSpec(memory_space=pltpu.SMEM),
            pl.BlockSpec(memory_space=pl.ANY),
        ],
        out_specs=pl.BlockSpec(memory_space=pltpu.VMEM),
        scratch_shapes=scratch,
        compiler_params=pltpu.CompilerParams(
            collective_id=0, has_side_effects=True, vmem_limit_bytes=60 << 20
        ),
        name="quegan",
    )(
        rowwise(swath_intensities, blocks * block_rows),
        destination_patch[:, 0],
        swath_leading_scanline,
        rowwise(receiver_floor_intensity, tile_rows),
    )
    return filtered.reshape(tile_rows, cols, pols, 128).transpose(0, 2, 1, 3).reshape(1, tile_rows, pols, width)


def solution(mesh):
    return jax.shard_map(
        per_device,
        mesh=mesh,
        in_specs=(
            P("date", "tile", None, None, None),
            P("tile", None),
            P("tile"),
            P("date", "tile", None, None),
        ),
        out_specs=P("date", "tile", None, None),
        check_vma=False,
    )
```

```python
import functools

import jax
import jax.numpy as jnp
from jax import lax
from jax.experimental import pallas as pl
from jax.experimental.pallas import tpu as pltpu
from jax.sharding import PartitionSpec as P

MESH = pl.DeviceIdType.MESH
RING = 4
BOUNDS = (0, 8, 24, 40, 56, 72, 88, 104, 120, 128)
LAGS = (0, 16, 64, 112, 152, 400)
LAG = 4
HALF = 3
GROUPS = (2, 1, 3, 0)
CHUNK = 16
FILTER_CHUNK = 4


def owner_of(first, second, core):
    x = first * (1 - core) + second * core
    z = second * (1 - core) + first * core
    return (x * RING + z) * 2 + core


def shift_columns(rows, by):
    lane = lax.broadcasted_iota(jnp.int32, rows.shape, 2)
    sub = lax.broadcasted_iota(jnp.int32, rows.shape, 1)
    turned = pltpu.roll(rows, by % 128, 2)
    if by > 0:
        beside = jnp.where(sub < 2, 0.0, pltpu.roll(turned, 2, 1))
        return jnp.where(lane < by, beside, turned)
    beside = jnp.where(sub >= 6, 0.0, pltpu.roll(turned, 6, 1))
    return jnp.where(lane >= 128 + by, beside, turned)


def kernel(
    blocks, block_rows, tile_rows, n_tile,
    swath, dest, lead, floor, out,
    raw, windows, table, xs, xr, as_, ar, b2s, b2r, bs, br, canvas, means, own_ratio, ds_, dr,
    raw_sem, table_sem, floor_sem, x_ss, x_rs, a_ss, a_rs, b2_ss, b2_rs, b_ss, b_rs, d_ss, d_rs,
):
    bf16, f32 = jnp.bfloat16, jnp.float32
    tile, date = lax.axis_index("tile"), lax.axis_index("date")
    core = tile % 2
    x, z = tile // (2 * RING), (tile // 2) % RING
    a = x * (1 - core) + z * core
    b = z * (1 - core) + x * core
    pieces = len(BOUNDS) - 1
    stride = tile_rows
    pad = stride - block_rows

    partner = (date, owner_of(b, a, 1 - core))
    ahead = (date, owner_of((a + 1) % RING, b, core))
    behind = (date, owner_of((a + RING - 1) % RING, b, core))
    across = [(date, owner_of(a, (b + j) % RING, core)) for j in (1, 2, 3)]
    dates = [((date + j) % RING, tile) for j in (1, 2, 3)]
    barrier = pltpu.get_barrier_semaphore()
    everyone = [partner, ahead, behind] + across + dates
    for device in everyone:
        pl.semaphore_signal(barrier, inc=1, device_id=device, device_id_type=MESH)

    loads = [
        pltpu.make_async_copy(
            swath.at[pl.ds(i * block_rows, block_rows)],
            raw.at[pl.ds(i * stride + pad, block_rows)],
            raw_sem.at[i],
        )
        for i in range(blocks)
    ]
    for copy in loads:
        copy.start()
    floor_copy = pltpu.make_async_copy(floor, canvas.at[pl.ds(HALF, tile_rows)], floor_sem)
    floor_copy.start()

    names = [dest[i] for i in range(blocks)]
    starts = [i * stride + pad - jnp.clip(lead[i], 0, pad) for i in range(blocks)]
    empty = blocks * stride

    owner = lax.broadcasted_iota(jnp.int32, (8, 128), 1)
    least = jnp.full((8, 128), empty, jnp.int32)
    other = least
    for i in range(blocks):
        here = jnp.where(owner == names[i], starts[i], empty)
        other = jnp.minimum(other, jnp.maximum(least, here))
        least = jnp.minimum(least, here)
    windows[0] = least
    windows[1] = other
    table_copy = pltpu.make_async_copy(windows, table, table_sem)
    table_copy.start()

    def clear(i, _):
        raw[pl.ds(i * stride, pad)] = jnp.zeros((pad, 8, 128), bf16)
        return 0

    lax.fori_loop(0, blocks, clear, 0)
    raw[pl.ds(blocks * stride, tile_rows)] = jnp.zeros((tile_rows, 8, 128), bf16)
    canvas[pl.ds(0, HALF)] = jnp.zeros((HALF, 8, 128), f32)
    canvas[pl.ds(HALF + tile_rows, HALF)] = jnp.zeros((HALF, 8, 128), f32)

    table_copy.wait()
    for copy in loads:
        copy.wait()

    sent = []

    def send(src, dst, ss, rs, device):
        copy = pltpu.make_async_remote_copy(
            src_ref=src, dst_ref=dst, send_sem=ss, recv_sem=rs, device_id=device, device_id_type=MESH
        )
        copy.start()
        sent.append(copy)
        return copy

    def spread(first, count, p, owner, store):
        low, high = BOUNDS[p], BOUNDS[p + 1]
        chunk = min(CHUNK, high - low)
        chunks = (high - low) // chunk

        def one(i, _):
            j = first + i // chunks
            row = low + (i % chunks) * chunk
            o = owner(j)
            one_, two_ = table[0, 0, o], table[1, 0, o]
            total = raw[pl.ds(one_ + row, chunk)].astype(f32) + raw[pl.ds(two_ + row, chunk)].astype(f32)
            store(j, pl.ds(row, chunk), total)
            return 0

        lax.fori_loop(0, count * chunks, one, 0)

    x_copies, a_copies, b2_copies, b_copies, d_copies = {}, {}, {}, {}, {}

    def rows_of(p):
        return pl.ds(BOUNDS[p], BOUNDS[p + 1] - BOUNDS[p])

    def mine(step):
        return lambda j: owner_of((a + step) % RING, (b + j) % RING, core)

    def build_for_partner(p, groups):
        for g in groups:

            def keep(j, rows, total):
                xs[g, j, rows] = total.astype(bf16)

            step = GROUPS[g]
            spread(0, RING, p, lambda j: owner_of((b + step) % RING, (a + j) % RING, 1 - core), keep)

    def to_partner(p):
        for k, groups in enumerate(((0, 1, 2), (3,))):
            if p > 0:
                build_for_partner(p, groups)
            part, n = pl.ds(groups[0], len(groups)), p * 2 + k
            x_copies[p, k] = send(
                xs.at[part, :, rows_of(p)], xr.at[part, :, rows_of(p)], x_ss.at[n], x_rs.at[n], partner
            )

    def first_sends(p):
        x_copies[p, 0].wait_recv()
        for way, device in enumerate((ahead, behind)):
            for g, first in ((0, 2 * way), (1 + way, 2 - 2 * way)):

                def keep(j, rows, total):
                    as_[way, j, rows] = (total + xr[g, j, rows].astype(f32)).astype(bf16)

                spread(first, 2, p, mine(GROUPS[g]), keep)
            k = p * 2 + way
            a_copies[p, way] = send(
                as_.at[way, :, rows_of(p)], ar.at[way, :, rows_of(p)], a_ss.at[k], a_rs.at[k], device
            )

    def second_sends(p):
        for way, device in enumerate((ahead, behind)):
            g = 1 + way
            a_copies[p, way].wait_recv()

            def keep(j, rows, total):
                total = total + xr[g, j, rows].astype(f32) + ar[way, j, rows].astype(f32)
                b2s[j, rows] = total.astype(bf16)

            spread(2 * way, 2, p, mine(GROUPS[g]), keep)
            k = p * 2 + way
            part = pl.ds(2 * way, 2)
            b2_copies[p, way] = send(
                b2s.at[part, rows_of(p)], b2r.at[part, rows_of(p)], b2_ss.at[k], b2_rs.at[k], device
            )

    def cross(p):
        x_copies[p, 1].wait_recv()
        for way in range(2):
            b2_copies[p, way].wait_recv()

        def summed(j, rows, total):
            total = total + xr[3, j, rows].astype(f32)
            return total + ar[1 - j // 2, j, rows].astype(f32) + b2r[j, rows].astype(f32)

        def keep(j, rows, total):
            bs[j - 1, rows] = summed(j, rows, total).astype(bf16)

        def keep_own(j, rows, total):
            here = pl.ds(HALF + rows.start, rows.size)
            canvas[here] += summed(0, rows, total)

        for j in (2, 1, 3):
            spread(j, 1, p, mine(0), keep)
            k = p * 3 + j - 1
            b_copies[p, j] = send(
                bs.at[j - 1, rows_of(p)], br.at[j - 1, rows_of(p)], b_ss.at[k], b_rs.at[k], across[j - 1]
            )
        if p == 0:
            floor_copy.wait()
        spread(0, 1, p, mine(0), keep_own)

    def filtered_rows(p):
        low = max(0, BOUNDS[p] - LAG)
        high = tile_rows if p == pieces - 1 else BOUNDS[p + 1] - LAG
        return low, high

    def box(p):
        for j in (1, 2, 3):
            b_copies[p, j].wait_recv()
        low, high = BOUNDS[p], BOUNDS[p + 1]

        def add(i, _):
            row = low + i * step
            rows = pl.ds(row, step)
            canvas[pl.ds(HALF + row, step)] += (
                br[0, rows].astype(f32) + br[1, rows].astype(f32) + br[2, rows].astype(f32)
            )
            return 0

        step = min(CHUNK, high - low)
        lax.fori_loop(0, (high - low) // step, add, 0)
        low, high = filtered_rows(p)
        shape = (FILTER_CHUNK, 8, 128)
        column = (lax.broadcasted_iota(jnp.int32, shape, 1) // 2) * 128 + lax.broadcasted_iota(jnp.int32, shape, 2)
        last = 4 * 128 - 1
        wide = jnp.minimum(column + HALF, last) - jnp.maximum(column - HALF, 0) + 1
        wide = wide.astype(f32)

        def smooth(i, _):
            row = low + i * FILTER_CHUNK
            total = canvas[pl.ds(row, FILTER_CHUNK)]
            for k in range(1, 2 * HALF + 1):
                total = total + canvas[pl.ds(row + k, FILTER_CHUNK)]
            summed = total
            for k in range(1, HALF + 1):
                summed = summed + (shift_columns(total, k) + shift_columns(total, -k))
            at = row + lax.broadcasted_iota(jnp.int32, shape, 0)
            tall = jnp.minimum(at + HALF, tile_rows - 1) - jnp.maximum(at - HALF, 0) + 1
            mean = summed / (tall.astype(f32) * wide)
            ratio = canvas[pl.ds(row + HALF, FILTER_CHUNK)] / mean
            rows = pl.ds(row, FILTER_CHUNK)
            means[rows] = mean
            own_ratio[rows] = ratio
            ds_[rows] = ratio.astype(bf16)
            return 0

        lax.fori_loop(0, (high - low) // FILTER_CHUNK, smooth, 0)
        rows = pl.ds(low, high - low)
        for j in (2, 1, 3):
            k = p * 3 + j - 1
            d_copies[p, j] = send(ds_.at[rows], dr.at[j - 1, rows], d_ss.at[k], d_rs.at[k], dates[j - 1])

    def finish(p):
        for j in (1, 2, 3):
            d_copies[p, j].wait_recv()
        low, high = filtered_rows(p)

        def one(i, _):
            rows = pl.ds(low + i * FILTER_CHUNK, FILTER_CHUNK)
            total = own_ratio[rows] + dr[0, rows].astype(f32)
            total = total + (dr[1, rows].astype(f32) + dr[2, rows].astype(f32))
            out[rows] = (means[rows] * (total * (1.0 / RING))).astype(bf16)
            return 0

        lax.fori_loop(0, (high - low) // FILTER_CHUNK, one, 0)

    build_for_partner(0, range(RING))
    pl.semaphore_wait(barrier, len(everyone))
    stages = (to_partner, first_sends, second_sends, cross, box, finish)
    steps = [(BOUNDS[p + 1] + LAGS[s], s, p) for p in range(pieces) for s in range(len(stages))]
    steps.sort()
    for _, s, p in steps[:-1]:
        stages[s](p)
    for copy in sent[:-3]:
        copy.wait_send()
    finish(pieces - 1)
    for copy in sent[-3:]:
        copy.wait_send()


def per_device(swath_intensities, destination_patch, swath_leading_scanline, receiver_floor_intensity):
    _, blocks, block_rows, pols, width = swath_intensities.shape
    tile_rows = receiver_floor_intensity.shape[1]
    n_tile = lax.axis_size("tile")
    cols = width // 128

    def rowwise(array, rows):
        return array.reshape(rows, pols, cols, 128).transpose(0, 2, 1, 3).reshape(rows, pols * cols, 128)

    pieces = len(BOUNDS) - 1
    bf16, f32 = jnp.bfloat16, jnp.float32

    def buffer(*lead, dtype=bf16):
        return pltpu.VMEM((*lead, 8, 128), dtype)

    dma = pltpu.SemaphoreType.DMA
    scratch = [
        buffer(blocks * tile_rows + tile_rows),
        pltpu.VMEM((2, 8, 128), jnp.int32), pltpu.SMEM((2, 8, 128), jnp.int32),
        buffer(4, 4, tile_rows), buffer(4, 4, tile_rows),
        buffer(2, 4, tile_rows), buffer(2, 4, tile_rows),
        buffer(4, tile_rows), buffer(4, tile_rows),
        buffer(3, tile_rows), buffer(3, tile_rows),
        buffer(tile_rows + 2 * HALF, dtype=f32),
        buffer(tile_rows, dtype=f32), buffer(tile_rows, dtype=f32),
        buffer(tile_rows), buffer(3, tile_rows),
        dma((blocks,)), dma, dma,
        dma((pieces * 2,)), dma((pieces * 2,)),
        dma((pieces * 2,)), dma((pieces * 2,)),
        dma((pieces * 2,)), dma((pieces * 2,)),
        dma((pieces * 3,)), dma((pieces * 3,)),
        dma((pieces * 3,)), dma((pieces * 3,)),
    ]
    filtered = pl.pallas_call(
        functools.partial(kernel, blocks, block_rows, tile_rows, n_tile),
        out_shape=jax.ShapeDtypeStruct((tile_rows, pols * cols, 128), bf16),
        in_specs=[
            pl.BlockSpec(memory_space=pl.ANY),
            pl.BlockSpec(memory_space=pltpu.SMEM),
            pl.BlockSpec(memory_space=pltpu.SMEM),
            pl.BlockSpec(memory_space=pl.ANY),
        ],
        out_specs=pl.BlockSpec(memory_space=pltpu.VMEM),
        scratch_shapes=scratch,
        compiler_params=pltpu.CompilerParams(
            collective_id=0, has_side_effects=True, vmem_limit_bytes=60 << 20
        ),
        name="quegan",
    )(
        rowwise(swath_intensities, blocks * block_rows),
        destination_patch[:, 0],
        swath_leading_scanline,
        rowwise(receiver_floor_intensity, tile_rows),
    )
    return filtered.reshape(tile_rows, cols, pols, 128).transpose(0, 2, 1, 3).reshape(1, tile_rows, pols, width)


def solution(mesh):
    return jax.shard_map(
        per_device,
        mesh=mesh,
        in_specs=(
            P("date", "tile", None, None, None),
            P("tile", None),
            P("tile"),
            P("date", "tile", None, None),
        ),
        out_specs=P("date", "tile", None, None),
        check_vma=False,
    )
```

```python
import functools

import jax
import jax.numpy as jnp
from jax import lax
from jax.experimental import pallas as pl
from jax.experimental.pallas import tpu as pltpu
from jax.sharding import PartitionSpec as P

MESH = pl.DeviceIdType.MESH
RING = 4
BOUNDS = (0, 8, 24, 40, 56, 72, 88, 104, 120, 128)
LAGS = (0, 16, 64, 112, 152, 400)
LAG = 4
HALF = 3
GROUPS = (2, 1, 3, 0)
CHUNK = 16
FILTER_CHUNK = 4


def owner_of(first, second, core):
    x = first * (1 - core) + second * core
    z = second * (1 - core) + first * core
    return (x * RING + z) * 2 + core


def shift_columns(rows, by):
    lane = lax.broadcasted_iota(jnp.int32, rows.shape, 2)
    sub = lax.broadcasted_iota(jnp.int32, rows.shape, 1)
    turned = pltpu.roll(rows, by % 128, 2)
    if by > 0:
        beside = jnp.where(sub < 2, 0.0, pltpu.roll(turned, 2, 1))
        return jnp.where(lane < by, beside, turned)
    beside = jnp.where(sub >= 6, 0.0, pltpu.roll(turned, 6, 1))
    return jnp.where(lane >= 128 + by, beside, turned)


def kernel(
    blocks, block_rows, tile_rows, n_tile,
    swath, dest, lead, floor, out,
    raw, windows, table, xs, xr, as_, ar, b2s, b2r, bs, br, canvas, means, own_ratio, ds_, dr,
    raw_sem, table_sem, floor_sem, x_ss, x_rs, a_ss, a_rs, b2_ss, b2_rs, b_ss, b_rs, d_ss, d_rs,
):
    bf16, f32 = jnp.bfloat16, jnp.float32
    tile, date = lax.axis_index("tile"), lax.axis_index("date")
    core = tile % 2
    x, z = tile // (2 * RING), (tile // 2) % RING
    a = x * (1 - core) + z * core
    b = z * (1 - core) + x * core
    pieces = len(BOUNDS) - 1
    stride = tile_rows
    pad = stride - block_rows

    partner = (date, owner_of(b, a, 1 - core))
    ahead = (date, owner_of((a + 1) % RING, b, core))
    behind = (date, owner_of((a + RING - 1) % RING, b, core))
    across = [(date, owner_of(a, (b + j) % RING, core)) for j in (1, 2, 3)]
    dates = [((date + j) % RING, tile) for j in (1, 2, 3)]
    barrier = pltpu.get_barrier_semaphore()
    everyone = [partner, ahead, behind] + across + dates
    for device in everyone:
        pl.semaphore_signal(barrier, inc=1, device_id=device, device_id_type=MESH)

    loads = [
        pltpu.make_async_copy(
            swath.at[pl.ds(i * block_rows, block_rows)],
            raw.at[pl.ds(i * stride + pad, block_rows)],
            raw_sem.at[i],
        )
        for i in range(blocks)
    ]
    for copy in loads:
        copy.start()
    floor_copy = pltpu.make_async_copy(floor, canvas.at[pl.ds(HALF, tile_rows)], floor_sem)
    floor_copy.start()

    names = [dest[i] for i in range(blocks)]
    starts = [i * stride + pad - jnp.clip(lead[i], 0, pad) for i in range(blocks)]
    empty = blocks * stride

    owner = lax.broadcasted_iota(jnp.int32, (8, 128), 1)
    least = jnp.full((8, 128), empty, jnp.int32)
    other = least
    for i in range(blocks):
        here = jnp.where(owner == names[i], starts[i], empty)
        other = jnp.minimum(other, jnp.maximum(least, here))
        least = jnp.minimum(least, here)
    windows[0] = least
    windows[1] = other
    table_copy = pltpu.make_async_copy(windows, table, table_sem)
    table_copy.start()

    def clear(i, _):
        raw[pl.ds(i * stride, pad)] = jnp.zeros((pad, 8, 128), bf16)
        return 0

    lax.fori_loop(0, blocks, clear, 0)
    raw[pl.ds(blocks * stride, tile_rows)] = jnp.zeros((tile_rows, 8, 128), bf16)
    canvas[pl.ds(0, HALF)] = jnp.zeros((HALF, 8, 128), f32)
    canvas[pl.ds(HALF + tile_rows, HALF)] = jnp.zeros((HALF, 8, 128), f32)

    table_copy.wait()
    for copy in loads:
        copy.wait()

    sent = []

    def send(src, dst, ss, rs, device):
        copy = pltpu.make_async_remote_copy(
            src_ref=src, dst_ref=dst, send_sem=ss, recv_sem=rs, device_id=device, device_id_type=MESH
        )
        copy.start()
        sent.append(copy)
        return copy

    def spread(first, count, p, owner, store):
        low, high = BOUNDS[p], BOUNDS[p + 1]
        chunk = min(CHUNK, high - low)
        chunks = (high - low) // chunk

        def one(i, _):
            j = first + i // chunks
            row = low + (i % chunks) * chunk
            o = owner(j)
            one_, two_ = table[0, 0, o], table[1, 0, o]
            total = raw[pl.ds(one_ + row, chunk)].astype(f32) + raw[pl.ds(two_ + row, chunk)].astype(f32)
            store(j, pl.ds(row, chunk), total)
            return 0

        lax.fori_loop(0, count * chunks, one, 0)

    x_copies, a_copies, b2_copies, b_copies, d_copies = {}, {}, {}, {}, {}

    def rows_of(p):
        return pl.ds(BOUNDS[p], BOUNDS[p + 1] - BOUNDS[p])

    def mine(step):
        return lambda j: owner_of((a + step) % RING, (b + j) % RING, core)

    def build_for_partner(p, groups):
        for g in groups:

            def keep(j, rows, total):
                xs[g, j, rows] = total.astype(bf16)

            step = GROUPS[g]
            spread(0, RING, p, lambda j: owner_of((b + step) % RING, (a + j) % RING, 1 - core), keep)

    def to_partner(p):
        for k, groups in enumerate(((0, 1), (2, 3))):
            if p > 0:
                build_for_partner(p, groups)
            part, n = pl.ds(groups[0], len(groups)), p * 2 + k
            x_copies[p, k] = send(
                xs.at[part, :, rows_of(p)], xr.at[part, :, rows_of(p)], x_ss.at[n], x_rs.at[n], partner
            )

    def first_sends(p):
        for way, device in enumerate((ahead, behind)):
            x_copies[p, way].wait_recv()
            for g, first in ((0, 2 * way), (1 + way, 2 - 2 * way)):

                def keep(j, rows, total):
                    as_[way, j, rows] = (total + xr[g, j, rows].astype(f32)).astype(bf16)

                spread(first, 2, p, mine(GROUPS[g]), keep)
            k = p * 2 + way
            a_copies[p, way] = send(
                as_.at[way, :, rows_of(p)], ar.at[way, :, rows_of(p)], a_ss.at[k], a_rs.at[k], device
            )

    def second_sends(p):
        for way, device in enumerate((ahead, behind)):
            g = 1 + way
            a_copies[p, way].wait_recv()

            def keep(j, rows, total):
                total = total + xr[g, j, rows].astype(f32) + ar[way, j, rows].astype(f32)
                b2s[j, rows] = total.astype(bf16)

            spread(2 * way, 2, p, mine(GROUPS[g]), keep)
            k = p * 2 + way
            part = pl.ds(2 * way, 2)
            b2_copies[p, way] = send(
                b2s.at[part, rows_of(p)], b2r.at[part, rows_of(p)], b2_ss.at[k], b2_rs.at[k], device
            )

    def cross(p):
        for way in range(2):
            b2_copies[p, way].wait_recv()

        def summed(j, rows, total):
            total = total + xr[3, j, rows].astype(f32)
            return total + ar[1 - j // 2, j, rows].astype(f32) + b2r[j, rows].astype(f32)

        def keep(j, rows, total):
            bs[j - 1, rows] = summed(j, rows, total).astype(bf16)

        def keep_own(j, rows, total):
            here = pl.ds(HALF + rows.start, rows.size)
            canvas[here] += summed(0, rows, total)

        for j in (2, 1, 3):
            spread(j, 1, p, mine(0), keep)
            k = p * 3 + j - 1
            b_copies[p, j] = send(
                bs.at[j - 1, rows_of(p)], br.at[j - 1, rows_of(p)], b_ss.at[k], b_rs.at[k], across[j - 1]
            )
        if p == 0:
            floor_copy.wait()
        spread(0, 1, p, mine(0), keep_own)

    def filtered_rows(p):
        low = max(0, BOUNDS[p] - LAG)
        high = tile_rows if p == pieces - 1 else BOUNDS[p + 1] - LAG
        return low, high

    def box(p):
        for j in (1, 2, 3):
            b_copies[p, j].wait_recv()
        low, high = BOUNDS[p], BOUNDS[p + 1]

        def add(i, _):
            row = low + i * step
            rows = pl.ds(row, step)
            canvas[pl.ds(HALF + row, step)] += (
                br[0, rows].astype(f32) + br[1, rows].astype(f32) + br[2, rows].astype(f32)
            )
            return 0

        step = min(CHUNK, high - low)
        lax.fori_loop(0, (high - low) // step, add, 0)
        low, high = filtered_rows(p)
        shape = (FILTER_CHUNK, 8, 128)
        column = (lax.broadcasted_iota(jnp.int32, shape, 1) // 2) * 128 + lax.broadcasted_iota(jnp.int32, shape, 2)
        last = 4 * 128 - 1
        wide = jnp.minimum(column + HALF, last) - jnp.maximum(column - HALF, 0) + 1
        wide = wide.astype(f32)

        def smooth(i, _):
            row = low + i * FILTER_CHUNK
            total = canvas[pl.ds(row, FILTER_CHUNK)]
            for k in range(1, 2 * HALF + 1):
                total = total + canvas[pl.ds(row + k, FILTER_CHUNK)]
            summed = total
            for k in range(1, HALF + 1):
                summed = summed + (shift_columns(total, k) + shift_columns(total, -k))
            at = row + lax.broadcasted_iota(jnp.int32, shape, 0)
            tall = jnp.minimum(at + HALF, tile_rows - 1) - jnp.maximum(at - HALF, 0) + 1
            mean = summed / (tall.astype(f32) * wide)
            ratio = canvas[pl.ds(row + HALF, FILTER_CHUNK)] / mean
            rows = pl.ds(row, FILTER_CHUNK)
            means[rows] = mean
            own_ratio[rows] = ratio
            ds_[rows] = ratio.astype(bf16)
            return 0

        lax.fori_loop(0, (high - low) // FILTER_CHUNK, smooth, 0)
        rows = pl.ds(low, high - low)
        for j in (2, 1, 3):
            k = p * 3 + j - 1
            d_copies[p, j] = send(ds_.at[rows], dr.at[j - 1, rows], d_ss.at[k], d_rs.at[k], dates[j - 1])

    def finish(p):
        for j in (1, 2, 3):
            d_copies[p, j].wait_recv()
        low, high = filtered_rows(p)

        def one(i, _):
            rows = pl.ds(low + i * FILTER_CHUNK, FILTER_CHUNK)
            total = own_ratio[rows] + dr[0, rows].astype(f32)
            total = total + (dr[1, rows].astype(f32) + dr[2, rows].astype(f32))
            out[rows] = (means[rows] * (total * (1.0 / RING))).astype(bf16)
            return 0

        lax.fori_loop(0, (high - low) // FILTER_CHUNK, one, 0)

    build_for_partner(0, range(RING))
    pl.semaphore_wait(barrier, len(everyone))
    stages = (to_partner, first_sends, second_sends, cross, box, finish)
    steps = [(BOUNDS[p + 1] + LAGS[s], s, p) for p in range(pieces) for s in range(len(stages))]
    steps.sort()
    for _, s, p in steps[:-1]:
        stages[s](p)
    for copy in sent[:-3]:
        copy.wait_send()
    finish(pieces - 1)
    for copy in sent[-3:]:
        copy.wait_send()


def per_device(swath_intensities, destination_patch, swath_leading_scanline, receiver_floor_intensity):
    _, blocks, block_rows, pols, width = swath_intensities.shape
    tile_rows = receiver_floor_intensity.shape[1]
    n_tile = lax.axis_size("tile")
    cols = width // 128

    def rowwise(array, rows):
        return array.reshape(rows, pols, cols, 128).transpose(0, 2, 1, 3).reshape(rows, pols * cols, 128)

    pieces = len(BOUNDS) - 1
    bf16, f32 = jnp.bfloat16, jnp.float32

    def buffer(*lead, dtype=bf16):
        return pltpu.VMEM((*lead, 8, 128), dtype)

    dma = pltpu.SemaphoreType.DMA
    scratch = [
        buffer(blocks * tile_rows + tile_rows),
        pltpu.VMEM((2, 8, 128), jnp.int32), pltpu.SMEM((2, 8, 128), jnp.int32),
        buffer(4, 4, tile_rows), buffer(4, 4, tile_rows),
        buffer(2, 4, tile_rows), buffer(2, 4, tile_rows),
        buffer(4, tile_rows), buffer(4, tile_rows),
        buffer(3, tile_rows), buffer(3, tile_rows),
        buffer(tile_rows + 2 * HALF, dtype=f32),
        buffer(tile_rows, dtype=f32), buffer(tile_rows, dtype=f32),
        buffer(tile_rows), buffer(3, tile_rows),
        dma((blocks,)), dma, dma,
        dma((pieces * 2,)), dma((pieces * 2,)),
        dma((pieces * 2,)), dma((pieces * 2,)),
        dma((pieces * 2,)), dma((pieces * 2,)),
        dma((pieces * 3,)), dma((pieces * 3,)),
        dma((pieces * 3,)), dma((pieces * 3,)),
    ]
    filtered = pl.pallas_call(
        functools.partial(kernel, blocks, block_rows, tile_rows, n_tile),
        out_shape=jax.ShapeDtypeStruct((tile_rows, pols * cols, 128), bf16),
        in_specs=[
            pl.BlockSpec(memory_space=pl.ANY),
            pl.BlockSpec(memory_space=pltpu.SMEM),
            pl.BlockSpec(memory_space=pltpu.SMEM),
            pl.BlockSpec(memory_space=pl.ANY),
        ],
        out_specs=pl.BlockSpec(memory_space=pltpu.VMEM),
        scratch_shapes=scratch,
        compiler_params=pltpu.CompilerParams(
            collective_id=0, has_side_effects=True, vmem_limit_bytes=60 << 20
        ),
        name="quegan",
    )(
        rowwise(swath_intensities, blocks * block_rows),
        destination_patch[:, 0],
        swath_leading_scanline,
        rowwise(receiver_floor_intensity, tile_rows),
    )
    return filtered.reshape(tile_rows, cols, pols, 128).transpose(0, 2, 1, 3).reshape(1, tile_rows, pols, width)


def solution(mesh):
    return jax.shard_map(
        per_device,
        mesh=mesh,
        in_specs=(
            P("date", "tile", None, None, None),
            P("tile", None),
            P("tile"),
            P("date", "tile", None, None),
        ),
        out_specs=P("date", "tile", None, None),
        check_vma=False,
    )
```
